256 devices in a mesh: layer: 16 (over y, x_hi, core), latent: 16 (over z, x_lo).
Axes of the slice: x: 4 (x_hi: 2, x_lo: 2; x = x_hi * 2 + x_lo), y: 4, z: 8, core: 2. Of those that a mesh axis runs over, the one named last changes fastest.
Arguments:
- activations: bfloat16 [16, 640, 8192], P('layer', None, 'latent'), may hold values from -24 to 24
- enc_weight: bfloat16 [16, 8192, 2048], P('layer', None, 'latent'), may hold values from -0.015625 to 0.015625
- enc_bias: float32 [2048], P('latent'), may hold values from -3 to 3
- dec_weight: bfloat16 [2048, 16, 8192], P('latent', 'layer'), may hold values from -0.125 to 0.125
- dec_bias: float32 [16, 8192], P('layer', 'latent'), may hold values from -3 to 3
Outputs:
- objective: float32 [], replicated
- grad_enc: bfloat16 [16, 8192, 2048], P('layer', None, 'latent')
- grad_enc_bias: float32 [2048], P('latent')
- grad_dec: bfloat16 [2048, 16, 8192], P('latent', 'layer')
- grad_dec_bias: float32 [16, 8192], P('layer', 'latent')
The draws below stay inside these ranges and needn't reach their ends.
All inputs are finite; a program needn't handle non-finite values.
Results may differ from the reference program's by a relative error of at most 0.0055.
Values may be sent and summed in bfloat16 or wider, within the bound.
No kernel may reach another device: no remote copies, remote signals or barrier semaphores. Data moves between devices by JAX's collectives and lax.ppermute only.
A program may use at most 128 MiB of HBM per device.

```python
import jax
import jax.numpy as jnp
from jax import lax

D = 8192
M = 2048
TOKENS = 640
LAYERS = 16


def draw_activations(key, part):
    key = jax.random.fold_in(key, 11)
    key_base, key_feat = jax.random.split(key, 2)
    depth = jnp.arange(LAYERS, dtype=jnp.float32) / max(LAYERS - 1, 1)
    layer_scale = 0.5 * jnp.power(4.0, depth)
    feat_scale = jax.random.uniform(key_feat, (D,), jnp.float32, 0.5, 2.0)
    base = jnp.clip(jax.random.normal(key_base, (LAYERS, TOKENS, D), jnp.float32), -6.0, 6.0)
    return (base * layer_scale[:, None, None] * feat_scale[None, None, :]).astype(jnp.bfloat16)


def shard_levels(rng, shape, shards, low, high):
    def one(dim, parts):
        steps = jax.random.uniform(jax.random.fold_in(jax.random.fold_in(rng, 6), dim), (parts,), jnp.float32, low / len(shards), high / len(shards))
        return jnp.repeat(jnp.exp(steps), shape[dim] // parts).reshape((-1,) + (1,) * (len(shape) - dim - 1))

    loudness = one(*shards[0])
    for cut in shards[1:]:
        loudness = loudness * one(*cut)
    return loudness


def normal_values(own_key, shape, spread, bound, cuts=(), kind=jnp.bfloat16):
    loudness = shard_levels(own_key, shape, cuts, -0.22, 0.18) if cuts else 1.0
    array = jax.random.normal(own_key, shape, jnp.float32) * spread * loudness
    return jnp.minimum(jnp.maximum(array, -bound), bound).astype(kind)


def setup_inputs(seed: int = 0) -> dict:
    streams_of = jax.random.split(jax.random.key(seed), 6)
    activations = draw_activations(jax.random.fold_in(streams_of[5], 71), 0)
    enc_weight = normal_values(streams_of[1], (LAYERS, D, M), (LAYERS * D) ** -0.5, 0.015625, ((0, 16), (2, 16)))
    enc_bias = normal_values(streams_of[2], (M,), 0.5, 3.0, ((0, 16),), jnp.float32)
    dec_weight = normal_values(streams_of[3], (M, LAYERS, D), M ** -0.5, 0.125, ((0, 16), (1, 16)))
    dec_bias = normal_values(streams_of[4], (LAYERS, D), 0.5, 3.0, ((0, 16), (1, 16)), jnp.float32)
    return {"activations": activations, "enc_weight": enc_weight, "enc_bias": enc_bias, "dec_weight": dec_weight, "dec_bias": dec_bias}


SHARPNESS = 4.0
PENALTY_WEIGHT = 4.0
EPSILON = 1e-06

def reference(activations, enc_weight, enc_bias, dec_weight, dec_bias):

    def enc_step(running, layer_pair):
        return (running + jnp.dot(layer_pair[0], layer_pair[1], preferred_element_type=jnp.float32), None)
    summed, _ = lax.scan(enc_step, jnp.zeros((TOKENS, M), jnp.float32), (activations, enc_weight))
    preact = summed + enc_bias[None, :]
    squash = jax.nn.sigmoid(SHARPNESS * preact)
    feature = preact * squash
    feature_low = feature.astype(jnp.bfloat16)
    wide_dec = dec_weight.astype(jnp.float32)
    norm_rows = jnp.sqrt(lax.optimization_barrier(jnp.sum(wide_dec * wide_dec, axis=2)) + EPSILON)
    feature_mass = lax.optimization_barrier(jnp.sum(feature, axis=0))

    def dec_step(running, layer_items):
        acts_layer, weight_layer, bias_layer = layer_items
        rebuilt = jnp.dot(feature_low, weight_layer, preferred_element_type=jnp.float32) + bias_layer[None, :]
        error_field = rebuilt - acts_layer.astype(jnp.float32)
        error_scaled = (2.0 / TOKENS * error_field).astype(jnp.bfloat16)
        grad_layer = jnp.dot(feature_low.T, error_scaled, preferred_element_type=jnp.float32)
        grad_feat = jnp.dot(error_scaled, weight_layer.T, preferred_element_type=jnp.float32)
        bias_grad = lax.optimization_barrier(jnp.sum(2.0 / TOKENS * error_field, axis=0))
        return (running + grad_feat, (grad_layer, bias_grad, jnp.sum(error_field * error_field)))
    grad_data, (grad_layers, grad_dec_bias, error_sums) = lax.scan(dec_step, jnp.zeros((TOKENS, M), jnp.float32), (activations, jnp.swapaxes(dec_weight, 0, 1), dec_bias))
    penalty_grad = PENALTY_WEIGHT / TOKENS * feature_mass[:, None, None] * wide_dec / norm_rows[:, :, None]
    grad_dec = (jnp.swapaxes(grad_layers, 0, 1) + penalty_grad).astype(jnp.bfloat16)
    norm_sum = lax.optimization_barrier(jnp.sum(norm_rows, axis=1))
    grad_feature = grad_data + PENALTY_WEIGHT / TOKENS * norm_sum[None, :]
    grad_preact = grad_feature * (squash + SHARPNESS * preact * squash * (1.0 - squash))
    grad_enc_bias = lax.optimization_barrier(jnp.sum(grad_preact, axis=0))
    grad_low = grad_preact.astype(jnp.bfloat16)

    def enc_grad(running, acts_layer):
        return (running, jnp.dot(acts_layer.T, grad_low, preferred_element_type=jnp.float32).astype(jnp.bfloat16))
    _, grad_enc = lax.scan(enc_grad, jnp.float32(0.0), activations)
    objective = (jnp.sum(error_sums) + PENALTY_WEIGHT * jnp.sum(feature * norm_sum[None, :])) / TOKENS
    return (objective, grad_enc, grad_enc_bias, grad_dec, grad_dec_bias)
```

```python
import jax
import jax.numpy as jnp
from jax import lax
from jax.sharding import Mesh, PartitionSpec as P

SHARPNESS = 4.0
PENALTY_WEIGHT = 4.0
EPSILON = 1e-06

LAYER = ("y", "xh", "core")
LATENT = ("z", "xl")
SPLIT = ("core", "y", "xh")
BF16 = jnp.bfloat16
F32 = jnp.float32


def ring(size, step):
    return [(i, (i + step) % size) for i in range(size)]


def shift(value, axis, step):
    return lax.ppermute(value, axis, ring(lax.axis_size(axis), step))


def gather_acts(own):
    half = own.shape[0] // 2
    other = shift(own, "xl", 1)
    found = {(0, 0): own, (0, 1): other}
    up = down = own
    tops, bottoms = {}, {}
    ups, downs = [], []
    for k in range(1, 4):
        up, down = shift(up, "z", 1), shift(down, "z", -1)
        found[-k, 0], found[k, 0] = up, down
        ups.append(up)
        downs.append(down)
    up4, down4 = shift(up[:half], "z", 1), shift(down[half:], "z", -1)
    for k in range(1, 4):
        tops[-k] = shift(ups[k - 1][:half], "xl", 1)
        bottoms[k] = shift(downs[k - 1][half:], "xl", 1)
    top4, bottom4 = shift(up4, "xl", 1), shift(down4, "xl", 1)
    low, high = other[half:], other[:half]
    for k in range(1, 4):
        low, high = shift(low, "z", 1), shift(high, "z", -1)
        bottoms[-k], tops[k] = low, high
    for k in (-1, 1, -2, 2, -3, 3):
        found[k, 1] = jnp.concatenate([tops[k], bottoms[k]])
    found[4, 0] = jnp.concatenate([up4, down4])
    found[4, 1] = jnp.concatenate([top4, bottom4])
    return found


def split3(value):
    high = lax.reduce_precision(value, 8, 7)
    rest = value - high
    middle = lax.reduce_precision(rest, 8, 7)
    return [v.astype(BF16) for v in (high, middle, rest - middle)]


def swap(blocks, axes):
    return lax.all_to_all(blocks, axes, 0, 0, tiled=True)


def spread(block, axes, count):
    return swap(jnp.broadcast_to(block[None], (count, *block.shape)), axes)


def gather_rows(block):
    pair = jnp.stack([block, shift(block, "xh", 1)])
    up, down = shift(pair, "y", 1), shift(pair, "y", -1)
    far = jnp.stack([shift(up[0], "y", 1), shift(down[1], "y", -1)])
    mine = jnp.stack([pair, up, down, far])
    theirs = shift(mine, "core", 1)
    y, xh, core = (lax.axis_index(a) for a in ("y", "xh", "core"))
    both = jnp.stack([mine, theirs])
    order = jnp.array([0, 2, 3, 1])[(jnp.arange(4) - y) % 4]
    both = both[(jnp.arange(2) - core) % 2][:, order][:, :, (jnp.arange(2) - xh) % 2]
    return both.reshape(16 * block.shape[0], block.shape[1])


def body(activations, enc_weight, enc_bias, dec_weight, dec_bias):
    tokens, width = activations.shape[1:]
    latents = enc_weight.shape[2]
    share = tokens // 16
    pad = 8
    own = activations[0]
    enc = enc_weight[0]
    dec = dec_weight[:, 0]
    z, xl = lax.axis_index("z"), lax.axis_index("xl")

    found = gather_acts(own)
    places = {(dz, dx): (((z + dz) % 8) * 2 + (xl + dx) % 2) * width for dz, dx in found}
    partial_value = jnp.zeros((tokens, latents), F32)
    for key, chunk in found.items():
        rows = lax.dynamic_slice_in_dim(enc, places[key], width, 0)
        partial_value += jnp.dot(chunk, rows, preferred_element_type=F32)

    wide = dec.astype(F32)
    norm = jnp.sqrt(jnp.sum(wide * wide, axis=1) + EPSILON)
    parts = jnp.concatenate(
        [
            partial_value.reshape(16, share, latents),
            jnp.broadcast_to(norm[None, None], (16, pad, latents)),
        ],
        axis=1,
    )
    summed = jnp.sum(swap(parts, SPLIT), axis=0)
    norm_sum = summed[share]
    preact = summed[:share] + enc_bias[None, :]
    squash = jax.nn.sigmoid(SHARPNESS * preact)
    feature = preact * squash
    penalty = jnp.sum(feature * norm_sum[None, :])

    block = jnp.concatenate(
        [feature.astype(BF16), jnp.stack(split3(norm)), jnp.zeros((pad - 3, latents), BF16)]
    )
    columns = spread(block, LATENT, 16)
    norm_rows = jnp.sum(columns[:, share : share + 3].astype(F32), axis=1).reshape(-1)
    columns = jnp.swapaxes(columns[:, :share], 0, 1).reshape(share, 16 * latents)
    features = gather_rows(columns)

    dec_all = lax.all_to_all(dec, LATENT, 1, 0, tiled=True)
    rebuilt = jnp.dot(features, dec_all, preferred_element_type=F32)
    error_field = rebuilt + dec_bias - own.astype(F32)
    scaled_wide = 2.0 / tokens * error_field
    error_scaled = scaled_wide.astype(BF16)
    grad_dec_bias = jnp.sum(scaled_wide, axis=0)[None]
    error_sum = jnp.sum(error_field * error_field)

    grad_part = lax.dot_general(
        error_scaled, dec_all, (((1,), (1,)), ((), ())), preferred_element_type=F32
    )
    mass = jnp.sum(features.astype(F32), axis=0)
    grad_data = lax.dot_general(
        features, error_scaled, (((0,), (0,)), ((), ())), preferred_element_type=F32
    )
    grad_dec = (
        grad_data + (PENALTY_WEIGHT / tokens * mass / norm_rows)[:, None] * dec_all.astype(F32)
    ).astype(BF16)
    grad_dec = lax.all_to_all(grad_dec, LATENT, 0, 1, tiled=True)[:, None]

    core = lax.axis_index("core")
    halves = grad_part.reshape(2, tokens // 2, 16 * latents)
    keep = lax.dynamic_index_in_dim(halves, core, 0, keepdims=False)
    give = lax.dynamic_index_in_dim(halves, 1 - core, 0, keepdims=False)
    mine = keep + shift(give, "core", 1)
    mine = jnp.sum(swap(mine.reshape(8, share, 16 * latents), ("y", "xh")), axis=0)
    loss = (error_sum + PENALTY_WEIGHT * penalty) / tokens
    mine = jnp.concatenate(
        [
            jnp.swapaxes(mine.reshape(share, 16, latents), 0, 1),
            jnp.broadcast_to(loss, (16, pad, latents)),
        ],
        axis=1,
    )
    mine = jnp.sum(swap(mine, LATENT), axis=0)
    grad_feature = mine[:share] + PENALTY_WEIGHT / tokens * norm_sum[None, :]
    grad_preact = grad_feature * (squash + SHARPNESS * preact * squash * (1.0 - squash))
    block = jnp.concatenate(
        [
            grad_preact.astype(BF16),
            jnp.stack(split3(jnp.sum(grad_preact, axis=0)) + split3(mine[share])),
            jnp.zeros((pad - 6, latents), BF16),
        ]
    )
    block = spread(block, SPLIT, 16)
    sums = jnp.sum(block[:, share:].astype(F32), axis=0)
    grad_enc_bias = sums[0] + sums[1] + sums[2]
    objective = (sums[3] + sums[4] + sums[5])[0]
    grad_low = block[:, :share].reshape(tokens, latents)
    grad_enc = jnp.zeros((16 * width, latents), BF16)
    for key, chunk in found.items():
        rows = lax.dot_general(
            chunk, grad_low, (((0,), (0,)), ((), ())), preferred_element_type=F32
        ).astype(BF16)
        grad_enc = lax.dynamic_update_slice_in_dim(grad_enc, rows, places[key], 0)
    return objective, grad_enc[None], grad_enc_bias, grad_dec, grad_dec_bias


def solution(mesh):
    fine = Mesh(mesh.devices.reshape(4, 2, 2, 8, 2), LAYER + LATENT)
    placed = (
        P(LAYER, None, LATENT),
        P(LAYER, None, LATENT),
        P(LATENT),
        P(LATENT, LAYER, None),
        P(LAYER, LATENT),
    )
    return jax.shard_map(
        body,
        mesh=fine,
        in_specs=placed,
        out_specs=(
            P(),
            P(LAYER, None, LATENT),
            P(LATENT),
            P(LATENT, LAYER, None),
            P(LAYER, LATENT),
        ),
        check_vma=False,
    )
```

```python
import functools

import jax
import jax.numpy as jnp
from jax import lax
from jax.experimental import pallas as pl
from jax.experimental.pallas import tpu as pltpu
from jax.sharding import Mesh, PartitionSpec as P

SHARPNESS = 4.0
PENALTY_WEIGHT = 4.0
EPSILON = 1e-06

LAYER = ("y", "xh", "core")
LATENT = ("z", "xl")
BF16 = jnp.bfloat16
F32 = jnp.float32


def after(value, *others):
    return lax.optimization_barrier((value, *others))[0]


def shift(value, axis, step):
    size = lax.axis_size(axis)
    return lax.ppermute(value, axis, [(i, (i + step) % size) for i in range(size)])


def partner(value, axis, bit):
    size = lax.axis_size(axis)
    return lax.ppermute(value, axis, [(i, i ^ bit) for i in range(size)])


def bit_of(axis, bit):
    return (lax.axis_index(axis) // bit) % 2


def double(value, axis, bit, dim):
    other = partner(value, axis, bit)
    first = bit_of(axis, bit) == 0
    return jnp.stack([jnp.where(first, value, other), jnp.where(first, other, value)], axis=dim)


def halve(value, axis, bit, dim):
    here = bit_of(axis, bit)
    give = lax.dynamic_index_in_dim(value, 1 - here, dim, keepdims=False)
    keep = lax.dynamic_index_in_dim(value, here, dim, keepdims=False)
    return keep + partner(give, axis, bit)


def scatter_y(blocks, kind):
    total = blocks[0].astype(F32)
    for k in (2, 1, 3):
        total += shift(blocks[k].astype(kind), "y", k).astype(F32)
    return total


def gather_y(block):
    far = shift(block, "y", -2)
    return jnp.concatenate([block, shift(block, "y", -1), far, shift(block, "y", -3)])


def split3(value):
    high = lax.reduce_precision(value, 8, 7)
    rest = value - high
    middle = lax.reduce_precision(rest, 8, 7)
    return [v.astype(BF16) for v in (high, middle, rest - middle)]


def own_kernel(share, place_ref, acts_ref, rows_ref, turned_ref):
    core, y = place_ref[0], place_ref[1]
    for i in range(8):
        c, k = i // 4, i % 4
        source = ((core + c) % 2 * 4 + (y + k) % 4) * share
        rows_ref[i * share : (i + 1) * share, :] = acts_ref[
            pl.ds(pl.multiple_of(source, share), share), :
        ]
    turned_ref[...] = rows_ref[...].T


def arrange_own(own, core, y):
    tokens, width = own.shape
    return pl.pallas_call(
        functools.partial(own_kernel, tokens // 8),
        in_specs=[
            pl.BlockSpec(memory_space=pltpu.SMEM),
            pl.BlockSpec(memory_space=pltpu.VMEM),
        ],
        out_shape=(
            jax.ShapeDtypeStruct((tokens, width), BF16),
            jax.ShapeDtypeStruct((width, tokens), BF16),
        ),
        name="arrange_own",
    )(jnp.stack([core, y]).astype(jnp.int32), own)


def cut_kernel(dec_ref, left_ref, right_ref):
    half = left_ref.shape[2]
    for i in range(4):
        left_ref[i] = dec_ref[:, 2 * i * half : (2 * i + 1) * half]
        right_ref[i] = dec_ref[:, (2 * i + 1) * half : (2 * i + 2) * half]


def cut_dec(dec, width):
    latents, depth = dec.shape
    count, half = depth // width, width // 2
    piece = pl.BlockSpec((4, latents, half), lambda j: (j, 0, 0))
    shape = jax.ShapeDtypeStruct((count, latents, half), BF16)
    return pl.pallas_call(
        cut_kernel,
        grid=(count // 4,),
        in_specs=[pl.BlockSpec((latents, 4 * width), lambda j: (0, j))],
        out_specs=(piece, piece),
        out_shape=(shape, shape),
        name="cut_dec",
    )(dec)


def join_kernel(left_ref, right_ref, out_ref):
    half = left_ref.shape[2]
    for i in range(4):
        out_ref[:, 2 * i * half : (2 * i + 1) * half] = left_ref[i]
        out_ref[:, (2 * i + 1) * half : (2 * i + 2) * half] = right_ref[i]


def join_dec(left, right):
    count, latents, half = left.shape
    piece = pl.BlockSpec((4, latents, half), lambda j: (j, 0, 0))
    return pl.pallas_call(
        join_kernel,
        grid=(count // 4,),
        in_specs=[piece, piece],
        out_specs=pl.BlockSpec((latents, 8 * half), lambda j: (0, j)),
        out_shape=jax.ShapeDtypeStruct((latents, count * 2 * half), BF16),
        name="join_dec",
    )(left, right)


def gather_acts(own, use, state):
    half = own.shape[0] // 2
    up, down = shift(own, "z", 1), shift(own, "z", -1)
    other = shift(own, "xl", 1)
    first = [(0, 0, 0, own), (-1, 0, 0, up), (1, 0, 0, down), (0, 1, 0, other)]
    low, high = other[half:], other[:half]

    def across(k, up, down):
        return [
            (-k, 1, 0, shift(up[:half], "xl", 1)),
            (k, 1, half, shift(down[half:], "xl", 1)),
        ]

    def beside(k, low, high):
        return [(-k, 1, half, low), (k, 1, 0, high)]

    pair = across(1, up, down)
    up, down = shift(up, "z", 1), shift(down, "z", -1)
    low, high = shift(low, "z", 1), shift(high, "z", -1)
    second = [(-2, 0, 0, up), (2, 0, 0, down), *beside(1, low, high)]
    state = use(state, first)
    up, down, low, high, state = lax.optimization_barrier((up, down, low, high, state))
    later = across(2, up, down)
    up, down = shift(up, "z", 1), shift(down, "z", -1)
    low, high = shift(low, "z", 1), shift(high, "z", -1)
    third = [(-3, 0, 0, up), (3, 0, 0, down), *beside(2, low, high)]
    state = use(state, second + pair)
    up, down, low, high, state = lax.optimization_barrier((up, down, low, high, state))
    last = across(3, up, down)
    far = [(4, 0, 0, shift(up[:half], "z", 1)), (4, 0, half, shift(down[half:], "z", -1))]
    low, high = shift(low, "z", 1), shift(high, "z", -1)
    state = use(state, third + later)
    low, high, state = lax.optimization_barrier((low, high, state))
    ends = [(4, 1, 0, shift(high, "z", -1)), (4, 1, half, shift(low, "z", 1))]
    state = use(state, far + beside(3, low, high) + last)
    state = use(state, ends)
    return state, [piece[3] for piece in far + ends]


def body(activations, enc_weight, enc_bias, dec_weight, dec_bias):
    tokens, width = activations.shape[1:]
    latents = enc_weight.shape[2]
    half, share = tokens // 2, tokens // 8
    small = share // 2
    pad = 8
    enc = enc_weight[0]
    dec = dec_weight[:, 0]
    z, xl, core, xh, y = (lax.axis_index(a) for a in ("z", "xl", "core", "xh", "y"))

    acts_here, turned = arrange_own(activations[0], core, y)

    def use(state, pieces):
        total, acts_all = state
        for dz, dx, row, chunk in pieces:
            place = (((z + dz) % 8) * 2 + (xl + dx) % 2) * width + row
            rows = lax.dynamic_slice_in_dim(enc, place, chunk.shape[0], 0)
            total += lax.dot_general(
                chunk, rows, (((0,), (0,)), ((), ())), preferred_element_type=F32
            )
            acts_all = lax.dynamic_update_slice_in_dim(acts_all, chunk, place, 0)
        return total, acts_all

    state = jnp.zeros((tokens, latents), F32), jnp.zeros((16 * width, tokens), BF16)
    (partial_value, acts_all), late = gather_acts(turned, use, state)
    dec_left, dec_right = cut_dec(dec, width)
    dec_left = after(dec_left, *late)
    dec_left = lax.all_to_all(dec_left, LATENT, 0, 0, tiled=True)

    wide = dec.astype(F32)
    norm = jnp.sqrt(jnp.sum(wide * wide, axis=1) + EPSILON)
    parts = jnp.concatenate(
        [
            partial_value.reshape(8, share, latents),
            jnp.broadcast_to(norm[None, None], (8, pad, latents)),
        ],
        axis=1,
    )
    summed = scatter_y(parts[:4] + partner(parts[4:], "core", 1), F32)
    summed += partner(summed, "xh", 1)
    norm_sum = summed[share]
    preact = summed[:share] + enc_bias[None, :]
    squash = jax.nn.sigmoid(SHARPNESS * preact)
    feature = preact * squash

    block = jnp.concatenate(
        [feature.astype(BF16), jnp.stack(split3(norm)), jnp.zeros((2 * pad - 3, latents), BF16)]
    )
    block = after(block, dec_left)
    block = double(block, "z", 4, 0)
    block = double(block, "z", 2, 1)
    block = double(block, "z", 1, 2)
    dec_right = after(dec_right, block)
    dec_right = lax.all_to_all(dec_right, LATENT, 0, 0, tiled=True)
    block = double(block, "xl", 1, 3).reshape(16, share + 2 * pad, latents)
    norm_rows = jnp.sum(block[:, share : share + 3].astype(F32), axis=1).reshape(-1)
    block = jnp.swapaxes(block[:, :share], 0, 1).reshape(share, -1)
    here = gather_y(block)
    features = (here, partner(here, "core", 1))
    mass = sum(jnp.sum(f.astype(F32), axis=0) for f in features)
    coef = (PENALTY_WEIGHT / tokens * mass / norm_rows)[:, None]

    transposed = (((1,), (1,)), ((), ()))
    summing = (((0,), (0,)), ((), ()))
    side = width // 2
    grads, biases, sums = [], [], []
    give = keep = None
    for i, part in enumerate((dec_left, dec_right)):
        part = part.reshape(16 * latents, side)
        columns = slice(i * side, (i + 1) * side)
        errors = []
        for j, f in enumerate(features):
            rebuilt = jnp.dot(f, part, preferred_element_type=F32)
            acts = acts_here[j * half : (j + 1) * half, columns].astype(F32)
            error_field = rebuilt + dec_bias[:, columns] - acts
            scaled_wide = 2.0 / tokens * error_field
            errors.append(scaled_wide.astype(BF16))
            biases.append(jnp.sum(scaled_wide, axis=0))
            sums.append(jnp.sum(error_field * error_field))
        products = [
            lax.dot_general(e, part, transposed, preferred_element_type=F32) for e in errors
        ]
        keep = products[0] if keep is None else keep + products[0]
        give = products[1] if give is None else give + products[1]
        grad = sum(
            lax.dot_general(f, e, summing, preferred_element_type=F32)
            for f, e in zip(features, errors)
        )
        grad = (grad + coef * part.astype(F32)).astype(BF16)
        grads.append(grad.reshape(16, latents, side))
    grad_dec_bias = jnp.concatenate([biases[0] + biases[1], biases[2] + biases[3]])[None]
    grad_left = lax.all_to_all(grads[0], LATENT, 0, 0, tiled=True)

    keep += partner(give, "core", 1)
    mine = scatter_y(keep.reshape(4, share, -1), BF16).reshape(2, small, -1)
    give = lax.dynamic_index_in_dim(mine, 1 - xh, 0, keepdims=False).astype(BF16)
    mine = lax.dynamic_index_in_dim(mine, xh, 0, keepdims=False)
    mine += partner(give, "xh", 1).astype(F32)

    def local(value):
        return lax.dynamic_slice_in_dim(value, xh * small, small, 0)

    preact, squash, feature = local(preact), local(squash), local(feature)
    penalty = jnp.sum(feature * norm_sum[None, :])
    loss = (sum(sums) + PENALTY_WEIGHT * penalty) / tokens
    mine = jnp.concatenate(
        [
            jnp.swapaxes(mine.reshape(small, 16, latents), 0, 1),
            jnp.broadcast_to(loss, (16, pad, latents)),
        ],
        axis=1,
    )
    mine = halve(mine.reshape(8, 2, small + pad, latents), "xl", 1, 1)
    mine = after(mine, grad_left)
    mine = halve(mine.reshape(4, 2, small + pad, latents), "z", 1, 1)
    mine = halve(mine.reshape(2, 2, small + pad, latents), "z", 2, 1)
    mine = halve(mine, "z", 4, 0)
    grad_right = after(grads[1], mine)
    grad_right = lax.all_to_all(grad_right, LATENT, 0, 0, tiled=True)
    grad_feature = mine[:small] + PENALTY_WEIGHT / tokens * norm_sum[None, :]
    grad_preact = grad_feature * (squash + SHARPNESS * preact * squash * (1.0 - squash))
    block = jnp.concatenate(
        [
            grad_preact.astype(BF16),
            jnp.stack(split3(jnp.sum(grad_preact, axis=0)) + split3(mine[small])),
            jnp.zeros((pad - 6, latents), BF16),
        ]
    )
    block = gather_y(double(block, "xh", 1, 0))
    block = jnp.concatenate([block, partner(block, "core", 1)])
    ends = block[:, small:].astype(F32).reshape(2, 4, 2, pad, latents)
    ends = jnp.where(core == 0, ends, ends[::-1])
    ends = lax.dynamic_slice_in_dim(jnp.concatenate([ends, ends], axis=1), (4 - y) % 4, 4, 1)
    ends = jnp.sum(ends.reshape(16, pad, latents), axis=0)
    grad_enc_bias = ends[0] + ends[1] + ends[2]
    objective = (ends[3] + ends[4] + ends[5])[0]
    grad_low = block[:, :small].reshape(tokens, latents)
    grad_enc = jnp.dot(acts_all, grad_low, preferred_element_type=F32).astype(BF16)
    grad_dec = join_dec(grad_left, grad_right)[:, None]
    return objective, grad_enc[None], grad_enc_bias, grad_dec, grad_dec_bias


def solution(mesh):
    fine = Mesh(mesh.devices.reshape(4, 2, 2, 8, 2), LAYER + LATENT)
    placed = (
        P(LAYER, None, LATENT),
        P(LAYER, None, LATENT),
        P(LATENT),
        P(LATENT, LAYER, None),
        P(LAYER, LATENT),
    )
    return jax.shard_map(
        body,
        mesh=fine,
        in_specs=placed,
        out_specs=(
            P(),
            P(LAYER, None, LATENT),
            P(LATENT),
            P(LATENT, LAYER, None),
            P(LAYER, LATENT),
        ),
        check_vma=False,
    )
```

```python
import functools

import jax
import jax.numpy as jnp
from jax import lax
from jax.experimental import pallas as pl
from jax.experimental.pallas import tpu as pltpu
from jax.sharding import Mesh, PartitionSpec as P

SHARPNESS = 4.0
PENALTY_WEIGHT = 4.0
EPSILON = 1e-06

LAYER = ("y", "xh", "core")
LATENT = ("z", "xl")
BF16 = jnp.bfloat16
F32 = jnp.float32


def after(value, *others):
    return lax.optimization_barrier((value, *others))[0]


def shift(value, axis, step):
    size = lax.axis_size(axis)
    return lax.ppermute(value, axis, [(i, (i + step) % size) for i in range(size)])


def partner(value, axis, bit):
    size = lax.axis_size(axis)
    return lax.ppermute(value, axis, [(i, i ^ bit) for i in range(size)])


def bit_of(axis, bit):
    return (lax.axis_index(axis) // bit) % 2


def double(value, axis, bit, dim, *along):
    other = after(partner(value, axis, bit), *along)
    first = bit_of(axis, bit) == 0
    return jnp.stack([jnp.where(first, value, other), jnp.where(first, other, value)], axis=dim)


def halve(value, axis, bit, dim):
    here = bit_of(axis, bit)
    give = lax.dynamic_index_in_dim(value, 1 - here, dim, keepdims=False)
    keep = lax.dynamic_index_in_dim(value, here, dim, keepdims=False)
    return keep + partner(give, axis, bit)


def scatter_y(blocks, kind, *along):
    total = blocks[0].astype(F32)
    came = [shift(blocks[k].astype(kind), "y", k) for k in (2, 1, 3)]
    came[0] = after(came[0], *along)
    for part in came:
        total += part.astype(F32)
    return total


def gather_y(block, *along):
    far, near, last = (shift(block, "y", -k) for k in (2, 1, 3))
    return jnp.concatenate([block, near, after(far, *along), last])


def split3(value):
    high = lax.reduce_precision(value, 8, 7)
    rest = value - high
    middle = lax.reduce_precision(rest, 8, 7)
    return [v.astype(BF16) for v in (high, middle, rest - middle)]


def own_kernel(share, place_ref, acts_ref, rows_ref, turned_ref):
    core, y = place_ref[0], place_ref[1]
    for i in range(8):
        c, k = i // 4, i % 4
        source = ((core + c) % 2 * 4 + (y + k) % 4) * share
        rows_ref[i * share : (i + 1) * share, :] = acts_ref[
            pl.ds(pl.multiple_of(source, share), share), :
        ]
    turned_ref[...] = rows_ref[...].T


def arrange_own(own, core, y):
    tokens, width = own.shape
    return pl.pallas_call(
        functools.partial(own_kernel, tokens // 8),
        in_specs=[
            pl.BlockSpec(memory_space=pltpu.SMEM),
            pl.BlockSpec(memory_space=pltpu.VMEM),
        ],
        out_shape=(
            jax.ShapeDtypeStruct((tokens, width), BF16),
            jax.ShapeDtypeStruct((width, tokens), BF16),
        ),
        name="arrange_own",
    )(jnp.stack([core, y]).astype(jnp.int32), own)


def cut_kernel(dec_ref, left_ref, right_ref):
    half = left_ref.shape[2]
    for i in range(4):
        left_ref[i] = dec_ref[:, 2 * i * half : (2 * i + 1) * half]
        right_ref[i] = dec_ref[:, (2 * i + 1) * half : (2 * i + 2) * half]


def cut_dec(dec, width):
    latents, depth = dec.shape
    count, half = depth // width, width // 2
    piece = pl.BlockSpec((4, latents, half), lambda j: (j, 0, 0))
    shape = jax.ShapeDtypeStruct((count, latents, half), BF16)
    return pl.pallas_call(
        cut_kernel,
        grid=(count // 4,),
        in_specs=[pl.BlockSpec((latents, 4 * width), lambda j: (0, j))],
        out_specs=(piece, piece),
        out_shape=(shape, shape),
        name="cut_dec",
    )(dec)


def join_kernel(left_ref, right_ref, out_ref):
    left, right = left_ref.shape[2], right_ref.shape[2]
    for i in range(4):
        start = i * (left + right)
        out_ref[:, start : start + left] = left_ref[i]
        out_ref[:, start + left : start + left + right] = right_ref[i]


def join_dec(left, right):
    count, latents, _ = left.shape
    width = left.shape[2] + right.shape[2]
    return pl.pallas_call(
        join_kernel,
        grid=(count // 4,),
        in_specs=[pl.BlockSpec((4, *a.shape[1:]), lambda j: (j, 0, 0)) for a in (left, right)],
        out_specs=pl.BlockSpec((latents, 4 * width), lambda j: (0, j)),
        out_shape=jax.ShapeDtypeStruct((latents, count * width), BF16),
        name="join_dec",
    )(left, right)


def decode_kernel(scale, features, left, right, acts, shift_ref, scaled, out, bias, squares):
    half, side = features.shape[0], left.shape[1]
    rows = half // 2
    bias[...] = jnp.zeros_like(bias)
    squares[...] = jnp.zeros_like(squares)
    for r in range(0, half, rows):
        lines = slice(r, r + rows)
        f = features[lines, :]
        products = []
        for i, part in enumerate((left, right)):
            columns = slice(i * side, (i + 1) * side)
            rebuilt = jnp.dot(f, part[...], preferred_element_type=F32)
            error = rebuilt + shift_ref[:, columns] - acts[lines, columns].astype(F32)
            wide = scale * error
            low = wide.astype(BF16)
            scaled[lines, columns] = low
            bias[:, columns] += jnp.sum(wide, axis=0, keepdims=True)
            squares[:, columns] += jnp.sum(error * error, axis=0, keepdims=True)
            products.append(
                lax.dot_general(
                    low, part[...], (((1,), (1,)), ((), ())), preferred_element_type=F32
                )
            )
        out[lines, :] = (products[0] + products[1]).astype(out.dtype)


def decode(features, parts, acts, shifts, tokens, kind):
    half, total = features.shape
    width = acts.shape[1]
    return pl.pallas_call(
        functools.partial(decode_kernel, 2.0 / tokens),
        out_shape=(
            jax.ShapeDtypeStruct((half, width), BF16),
            jax.ShapeDtypeStruct((half, total), kind),
            jax.ShapeDtypeStruct((1, width), F32),
            jax.ShapeDtypeStruct((1, width), F32),
        ),
        compiler_params=pltpu.CompilerParams(vmem_limit_bytes=48 * 1024 * 1024),
        cost_estimate=pl.CostEstimate(
            flops=4 * half * total * width,
            transcendentals=0,
            bytes_accessed=8 * half * total,
        ),
        name="decode",
    )(features, *parts, acts, shifts)


def gather_acts(own, slab, early, use, state):
    half = own.shape[0] // 2
    up, down = shift(own, "z", 1), shift(own, "z", -1)
    xl = lax.axis_index("xl")
    came = shift(lax.dynamic_index_in_dim(slab, 1 - xl, 1, keepdims=False), "xl", 1)
    first = [(0, 0, own), (-1, 0, up), (1, 0, down)]
    other = [(k, 0, shift(after(v, came), "xl", 1)) for k, _, v in first]
    up, down, *early = lax.optimization_barrier((up, down, *early))
    up, down = shift(up, "z", 1), shift(down, "z", -1)
    slab = lax.dynamic_index_in_dim(after(slab, came), xl, 1, keepdims=False)
    slab = jnp.concatenate([slab, came], axis=2)
    state = use(state, first, slab)
    second = [(-2, 0, up), (2, 0, down)]
    up, down, state = lax.optimization_barrier((up, down, state))
    up, down = shift(up, "z", 1), shift(down, "z", -1)
    state = use(state, second, slab)
    third = [(-3, 0, up), (3, 0, down)]
    up, down, state = lax.optimization_barrier((up, down, state))
    top, bottom = lax.optimization_barrier((up[:half], down[half:]))
    far = [(4, 0, shift(top, "z", 1)), (4, half, shift(bottom, "z", -1))]
    state = use(state, third, slab)
    state = use(state, far, slab, False)
    return state, first + second + third + far, other, early


def body(activations, enc_weight, enc_bias, dec_weight, dec_bias):
    tokens, width = activations.shape[1:]
    latents = enc_weight.shape[2]
    half, share = tokens // 2, tokens // 8
    small = share // 2
    pad = 8
    enc = enc_weight[0]
    dec = dec_weight[:, 0]
    z, xl, core, xh, y = (lax.axis_index(a) for a in ("z", "xl", "core", "xh", "y"))

    acts_here, turned = arrange_own(activations[0], core, y)
    def store(acts_all, pieces, column):
        for dz, row, chunk in pieces:
            place = (((z + dz) % 8) * 2 + column) * width + row
            acts_all = lax.dynamic_update_slice_in_dim(acts_all, chunk, place, 0)
        return acts_all

    def use(state, pieces, slab, keep=True):
        total, acts_all = state
        for dz, row, chunk in pieces:
            rows = lax.dynamic_index_in_dim(slab, (z + dz) % 8, 0, keepdims=False)
            rows = rows[row : row + chunk.shape[0]]
            total += lax.dot_general(
                chunk, rows, (((0,), (0,)), ((), ())), preferred_element_type=F32
            )
        return total, store(acts_all, pieces, xl) if keep else acts_all

    def cross(pieces, *others):
        return [(k, row, shift(after(v, *others), "xl", 1)) for k, row, v in pieces]

    wide = dec.astype(F32)
    norm = jnp.sqrt(jnp.sum(wide * wide, axis=1) + EPSILON)
    slab = after(enc, turned).reshape(8, 2, width, latents)
    state = jnp.zeros((tokens, 2 * latents), F32), jnp.zeros((16 * width, tokens), BF16)
    early = [*cut_dec(dec, width), norm]
    state, pieces, other, early = gather_acts(turned, slab, early, use, state)
    total, acts_all = state
    dec_left, dec_right, norm = early
    total = after(total, other[0][2], other[1][2])
    dec_left = after(dec_left, pieces[-1][2], pieces[-2][2])
    dec_left = lax.all_to_all(dec_left, LATENT, 0, 0, tiled=True)

    ends = jnp.concatenate([norm, jnp.zeros_like(norm)])
    parts = jnp.concatenate(
        [
            total.reshape(8, share, 2 * latents),
            jnp.broadcast_to(ends[None, None], (8, pad, 2 * latents)),
        ],
        axis=1,
    )
    summed = parts[:4] + partner(parts[4:], "core", 1)
    summed, acts_all, _ = lax.optimization_barrier((summed, acts_all, other[2][2]))
    acts_all = store(store(acts_all, pieces[7:], xl), other, 1 - xl)
    low = width // 2
    k, _, chunk = pieces[4]
    split = [(k, 0, chunk[:low]), (k, low, chunk[low:])]
    other = cross(pieces[3:4])
    summed = after(scatter_y(summed, F32), other[0][2])
    acts_all = store(acts_all, other, 1 - xl)
    mine, theirs = summed[:, :latents], summed[:, latents:]
    side_sum = mine + partner(theirs, "xl", 1)
    summed = side_sum + (partner(mine, "xh", 1) + partner(theirs, ("xh", "xl"), 3))
    norm_sum = summed[share]
    preact = summed[:share] + enc_bias[None, :]
    squash = jax.nn.sigmoid(SHARPNESS * preact)
    feature = preact * squash

    block = jnp.concatenate(
        [feature.astype(BF16), jnp.stack(split3(norm)), jnp.zeros((2 * pad - 3, latents), BF16)]
    )
    block, dec_left, acts_all = lax.optimization_barrier((block, dec_left, acts_all))
    block = jnp.broadcast_to(block[None], (8, *block.shape))
    other = cross(split[1:], block)
    block = after(lax.all_to_all(block, "z", 0, 0, tiled=True), other[0][2])
    acts_all = store(acts_all, other, 1 - xl)
    dec_right = after(dec_right, block)
    dec_right = lax.all_to_all(dec_right, LATENT, 0, 0, tiled=True)
    block = double(block, "xl", 1, 1).reshape(16, share + 2 * pad, latents)
    other = cross(pieces[5:6], block)
    norm_rows = jnp.sum(block[:, share : share + 3].astype(F32), axis=1).reshape(-1)
    block = jnp.swapaxes(block[:, :share], 0, 1).reshape(share, -1)
    here = gather_y(block)
    features = after(here, other[0][2]), partner(here, "core", 1)
    acts_all = store(acts_all, other, 1 - xl)
    mass = sum(jnp.sum(f.astype(F32), axis=0) for f in features)
    coef = (PENALTY_WEIGHT / tokens * mass / norm_rows)[:, None]

    side = width // 2
    parts = [part.reshape(16 * latents, side) for part in (dec_left, dec_right)]
    errors = [None, None]
    errors[1], give, bias, squares = decode(
        features[1], parts, acts_here[half:], dec_bias, tokens, BF16
    )
    errors[0], keep, more_bias, more_squares = decode(
        features[0], parts, acts_here[:half], dec_bias, tokens, F32
    )
    grad_dec_bias = more_bias + bias
    squares += more_squares
    keep += partner(give, "core", 1).astype(F32)
    keep, *errors = lax.optimization_barrier((keep, *errors))
    grads = []
    for i, part in enumerate(parts):
        grad = coef * part.astype(F32)
        for j, f in enumerate(features):
            error = errors[j][:, i * side : (i + 1) * side]
            grad += lax.dot_general(
                f, error, (((0,), (0,)), ((), ())), preferred_element_type=F32
            )
        grads.append(grad.astype(BF16).reshape(16, latents, side))
    grad_left = lax.all_to_all(grads[0], LATENT, 0, 0, tiled=True)

    other = cross([pieces[6], split[0]], keep)
    mine = scatter_y(keep.reshape(4, share, -1), BF16, other[0][2], other[1][2])
    mine = mine.reshape(2, small, -1)
    mine, acts_all = lax.optimization_barrier((mine, store(acts_all, other, 1 - xl)))
    give = lax.dynamic_index_in_dim(mine, 1 - xh, 0, keepdims=False).astype(BF16)
    mine = lax.dynamic_index_in_dim(mine, xh, 0, keepdims=False)
    mine += partner(give, "xh", 1).astype(F32)

    def local(value):
        return lax.dynamic_slice_in_dim(value, xh * small, small, 0)

    preact, squash, feature = local(preact), local(squash), local(feature)
    penalty = jnp.sum(feature * norm_sum[None, :])
    loss = (jnp.sum(squares) + PENALTY_WEIGHT * penalty) / tokens
    mine = jnp.concatenate(
        [
            jnp.swapaxes(mine.reshape(small, 16, latents), 0, 1),
            jnp.broadcast_to(loss, (16, pad, latents)),
        ],
        axis=1,
    )
    mine = halve(mine.reshape(8, 2, small + pad, latents), "xl", 1, 1)
    mine = after(mine, grad_left)
    other = cross(pieces[7:8], mine)
    mine = lax.all_to_all(mine, "z", 0, 0, tiled=True)
    mine = jnp.sum(after(mine, other[0][2]), axis=0)
    acts_all = store(acts_all, other, 1 - xl)
    grad_right = after(grads[1], mine)
    grad_right = lax.all_to_all(grad_right, LATENT, 0, 0, tiled=True)
    grad_feature = mine[:small] + PENALTY_WEIGHT / tokens * norm_sum[None, :]
    grad_preact = grad_feature * (squash + SHARPNESS * preact * squash * (1.0 - squash))
    block = jnp.concatenate(
        [
            grad_preact.astype(BF16),
            jnp.stack(split3(jnp.sum(grad_preact, axis=0)) + split3(mine[small])),
            jnp.zeros((pad - 6, latents), BF16),
        ]
    )
    other = cross(pieces[8:], mine)
    block = gather_y(double(block, "xh", 1, 0), other[0][2])
    acts_all = store(acts_all, other, 1 - xl)
    block = jnp.concatenate([block, partner(block, "core", 1)])
    ends = block[:, small:].astype(F32).reshape(2, 4, 2, pad, latents)
    ends = jnp.where(core == 0, ends, ends[::-1])
    ends = lax.dynamic_slice_in_dim(jnp.concatenate([ends, ends], axis=1), (4 - y) % 4, 4, 1)
    ends = jnp.sum(ends.reshape(16, pad, latents), axis=0)
    grad_enc_bias = ends[0] + ends[1] + ends[2]
    objective = (ends[3] + ends[4] + ends[5])[0]
    grad_low = block[:, :small].reshape(tokens, latents)
    grad_enc = jnp.dot(acts_all, grad_low, preferred_element_type=F32).astype(BF16)
    grad_dec = join_dec(grad_left, grad_right)[:, None]
    return objective, grad_enc[None], grad_enc_bias, grad_dec, grad_dec_bias


def solution(mesh):
    fine = Mesh(mesh.devices.reshape(4, 2, 2, 8, 2), LAYER + LATENT)
    placed = (
        P(LAYER, None, LATENT),
        P(LAYER, None, LATENT),
        P(LATENT),
        P(LATENT, LAYER, None),
        P(LAYER, LATENT),
    )
    return jax.shard_map(
        body,
        mesh=fine,
        in_specs=placed,
        out_specs=(
            P(),
            P(LAYER, None, LATENT),
            P(LATENT),
            P(LATENT, LAYER, None),
            P(LAYER, LATENT),
        ),
        check_vma=False,
    )
```

```python
import functools

import jax
import jax.numpy as jnp
from jax import lax
from jax.experimental import pallas as pl
from jax.experimental.pallas import tpu as pltpu
from jax.sharding import Mesh, PartitionSpec as P

SHARPNESS = 4.0
PENALTY_WEIGHT = 4.0
EPSILON = 1e-06

LAYER = ("y", "xh", "core")
LATENT = ("z", "xl")
BF16 = jnp.bfloat16
F32 = jnp.float32


def after(value, *others):
    return lax.optimization_barrier((value, *others))[0]


def shift(value, axis, step):
    size = lax.axis_size(axis)
    return lax.ppermute(value, axis, [(i, (i + step) % size) for i in range(size)])


def partner(value, axis, bit):
    size = lax.axis_size(axis)
    return lax.ppermute(value, axis, [(i, i ^ bit) for i in range(size)])


def bit_of(axis, bit):
    return (lax.axis_index(axis) // bit) % 2


def double(value, axis, bit, dim, *along):
    other = after(partner(value, axis, bit), *along)
    first = bit_of(axis, bit) == 0
    return jnp.stack([jnp.where(first, value, other), jnp.where(first, other, value)], axis=dim)


def halve(value, axis, bit, dim):
    here = bit_of(axis, bit)
    give = lax.dynamic_index_in_dim(value, 1 - here, dim, keepdims=False)
    keep = lax.dynamic_index_in_dim(value, here, dim, keepdims=False)
    return keep + partner(give, axis, bit)


def scatter_y(blocks, kind, *along):
    total = blocks[0].astype(F32)
    came = [shift(blocks[k].astype(kind), "y", k) for k in (2, 1, 3)]
    came[0] = after(came[0], *along)
    for part in came:
        total += part.astype(F32)
    return total


def gather_y(block, *along):
    far, near, last = (shift(block, "y", -k) for k in (2, 1, 3))
    return jnp.concatenate([block, near, after(far, *along), last])


def split3(value):
    high = lax.reduce_precision(value, 8, 7)
    rest = value - high
    middle = lax.reduce_precision(rest, 8, 7)
    return [v.astype(BF16) for v in (high, middle, rest - middle)]


def own_kernel(share, place_ref, acts_ref, rows_ref, turned_ref):
    core, y = place_ref[0], place_ref[1]
    for i in range(8):
        c, k = i // 4, i % 4
        source = ((core + c) % 2 * 4 + (y + k) % 4) * share
        rows_ref[i * share : (i + 1) * share, :] = acts_ref[
            pl.ds(pl.multiple_of(source, share), share), :
        ]
    turned_ref[...] = rows_ref[...].T


def arrange_own(own, core, y):
    tokens, width = own.shape
    return pl.pallas_call(
        functools.partial(own_kernel, tokens // 8),
        in_specs=[
            pl.BlockSpec(memory_space=pltpu.SMEM),
            pl.BlockSpec(memory_space=pltpu.VMEM),
        ],
        out_shape=(
            jax.ShapeDtypeStruct((tokens, width), BF16),
            jax.ShapeDtypeStruct((width, tokens), BF16),
        ),
        name="arrange_own",
    )(jnp.stack([core, y]).astype(jnp.int32), own)


def cut_kernel(dec_ref, left_ref, right_ref):
    half = left_ref.shape[2]
    for i in range(4):
        left_ref[i] = dec_ref[:, 2 * i * half : (2 * i + 1) * half]
        right_ref[i] = dec_ref[:, (2 * i + 1) * half : (2 * i + 2) * half]


def cut_dec(dec, width):
    latents, depth = dec.shape
    count, half = depth // width, width // 2
    piece = pl.BlockSpec((4, latents, half), lambda j: (j, 0, 0))
    shape = jax.ShapeDtypeStruct((count, latents, half), BF16)
    return pl.pallas_call(
        cut_kernel,
        grid=(count // 4,),
        in_specs=[pl.BlockSpec((latents, 4 * width), lambda j: (0, j))],
        out_specs=(piece, piece),
        out_shape=(shape, shape),
        name="cut_dec",
    )(dec)


def join_kernel(left_ref, right_ref, out_ref):
    count, _, side = left_ref.shape
    for i in range(count):
        start = 2 * i * side
        out_ref[:, start : start + side] = left_ref[i]
        out_ref[:, start + side : start + 2 * side] = right_ref[i]


def join_dec(left, right):
    count, latents, side = left.shape
    return pl.pallas_call(
        join_kernel,
        out_shape=jax.ShapeDtypeStruct((latents, 2 * count * side), BF16),
        compiler_params=pltpu.CompilerParams(vmem_limit_bytes=48 * 1024 * 1024),
        name="join_dec",
    )(left, right)


def rows_kernel(low_ref, *refs):
    start = 0
    for chunk_ref in refs[:-1]:
        count = chunk_ref.shape[0]
        rows = jnp.dot(chunk_ref[...], low_ref[...], preferred_element_type=F32)
        refs[-1][start : start + count, :] = rows.astype(BF16)
        start += count


def encode_rows(chunks, low):
    count = sum(chunk.shape[0] for chunk in chunks)
    return pl.pallas_call(
        rows_kernel,
        out_shape=jax.ShapeDtypeStruct((count, low.shape[1]), BF16),
        compiler_params=pltpu.CompilerParams(vmem_limit_bytes=48 * 1024 * 1024),
        name="encode_rows",
    )(low, *chunks)


def grad_enc_kernel(width, steps, place_ref, low_ref, *refs):
    z, xl = place_ref[0], place_ref[1]
    out_ref = refs[-1]
    for (dz, dx, row), chunk_ref in zip(steps, refs):
        place = ((z + dz + 8) % 8 * 2 + (xl + dx) % 2) * width + row
        count = chunk_ref.shape[0]
        rows = jnp.dot(chunk_ref[...], low_ref[...], preferred_element_type=F32)
        out_ref[pl.ds(pl.multiple_of(place, count), count), :] = rows.astype(BF16)


def encode_grad(z, xl, low, pieces, others, width):
    steps = [(dz, 0, row) for dz, row, _ in pieces] + [(dz, 1, row) for dz, row, _ in others]
    chunks = [piece[2] for piece in (*pieces, *others)]
    specs = [pl.BlockSpec(memory_space=pltpu.SMEM)]
    specs += [pl.BlockSpec(memory_space=pltpu.VMEM)] * (1 + len(chunks))
    return pl.pallas_call(
        functools.partial(grad_enc_kernel, width, steps),
        in_specs=specs,
        out_shape=jax.ShapeDtypeStruct((16 * width, low.shape[1]), BF16),
        compiler_params=pltpu.CompilerParams(vmem_limit_bytes=48 * 1024 * 1024),
        name="encode_grad",
    )(jnp.stack([z, xl]).astype(jnp.int32), low, *chunks)


def decode_kernel(scale, features, left, right, acts, shift_ref, scaled, out, bias, squares):
    half, side = features.shape[0], left.shape[1]
    rows = half // 2
    bias[...] = jnp.zeros_like(bias)
    squares[...] = jnp.zeros_like(squares)
    for r in range(0, half, rows):
        lines = slice(r, r + rows)
        f = features[lines, :]
        products = []
        for i, part in enumerate((left, right)):
            columns = slice(i * side, (i + 1) * side)
            rebuilt = jnp.dot(f, part[...], preferred_element_type=F32)
            error = rebuilt + shift_ref[:, columns] - acts[lines, columns].astype(F32)
            wide = scale * error
            low = wide.astype(BF16)
            scaled[lines, columns] = low
            bias[:, columns] += jnp.sum(wide, axis=0, keepdims=True)
            squares[:, columns] += jnp.sum(error * error, axis=0, keepdims=True)
            products.append(
                lax.dot_general(
                    low, part[...], (((1,), (1,)), ((), ())), preferred_element_type=F32
                )
            )
        out[lines, :] = (products[0] + products[1]).astype(out.dtype)


def decode(features, parts, acts, shifts, tokens, kind):
    half, total = features.shape
    width = acts.shape[1]
    return pl.pallas_call(
        functools.partial(decode_kernel, 2.0 / tokens),
        out_shape=(
            jax.ShapeDtypeStruct((half, width), BF16),
            jax.ShapeDtypeStruct((half, total), kind),
            jax.ShapeDtypeStruct((1, width), F32),
            jax.ShapeDtypeStruct((1, width), F32),
        ),
        compiler_params=pltpu.CompilerParams(vmem_limit_bytes=48 * 1024 * 1024),
        cost_estimate=pl.CostEstimate(
            flops=4 * half * total * width,
            transcendentals=0,
            bytes_accessed=8 * half * total,
        ),
        name="decode",
    )(features, *parts, acts, shifts)


def gather_acts(own, slab, early, use, state):
    half = own.shape[0] // 2
    up, down = shift(own, "z", 1), shift(own, "z", -1)
    xl = lax.axis_index("xl")
    came = shift(lax.dynamic_index_in_dim(slab, 1 - xl, 1, keepdims=False), "xl", 1)
    first = [(0, 0, own), (-1, 0, up), (1, 0, down)]
    other = [(k, 0, shift(after(v, came), "xl", 1)) for k, _, v in first]
    up, down, *early = lax.optimization_barrier((up, down, *early))
    up, down = shift(up, "z", 1), shift(down, "z", -1)
    slab = lax.dynamic_index_in_dim(after(slab, came), xl, 1, keepdims=False)
    slab = jnp.concatenate([slab, came], axis=2)
    state = use(state, first, slab)
    second = [(-2, 0, up), (2, 0, down)]
    up, down, state = lax.optimization_barrier((up, down, state))
    up, down = shift(up, "z", 1), shift(down, "z", -1)
    state = use(state, second, slab)
    third = [(-3, 0, up), (3, 0, down)]
    up, down, state = lax.optimization_barrier((up, down, state))
    top, bottom = lax.optimization_barrier((up[:half], down[half:]))
    far = [(4, 0, shift(top, "z", 1)), (4, half, shift(bottom, "z", -1))]
    state = use(state, third, slab)
    early[0] = after(early[0], state)
    state = use(state, far, slab)
    return state, first + second + third + far, other, early


def body(activations, enc_weight, enc_bias, dec_weight, dec_bias):
    tokens, width = activations.shape[1:]
    latents = enc_weight.shape[2]
    half, share = tokens // 2, tokens // 8
    small = share // 2
    pad = 8
    enc = enc_weight[0]
    dec = dec_weight[:, 0]
    z, xl, core, xh, y = (lax.axis_index(a) for a in ("z", "xl", "core", "xh", "y"))

    acts_here, turned = arrange_own(activations[0], core, y)
    def use(total, pieces, slab):
        for dz, row, chunk in pieces:
            rows = lax.dynamic_index_in_dim(slab, (z + dz) % 8, 0, keepdims=False)
            rows = rows[row : row + chunk.shape[0]]
            total += lax.dot_general(
                chunk, rows, (((0,), (0,)), ((), ())), preferred_element_type=F32
            )
        return total

    def cross(pieces, *others):
        return [(k, row, shift(after(v, *others), "xl", 1)) for k, row, v in pieces]

    wide = dec.astype(F32)
    norm = jnp.sqrt(jnp.sum(wide * wide, axis=1) + EPSILON)
    slab = after(enc, turned).reshape(8, 2, width, latents)
    total = jnp.zeros((tokens, 2 * latents), F32)
    early = [*cut_dec(dec, width), norm]
    total, pieces, other, early = gather_acts(turned, slab, early, use, total)
    others = list(other)
    dec_left, dec_right, norm = early
    total = after(total, other[0][2], other[1][2])
    dec_left = lax.all_to_all(dec_left, LATENT, 0, 0, tiled=True)

    ends = jnp.concatenate([norm, jnp.zeros_like(norm)])
    parts = jnp.concatenate(
        [
            total.reshape(8, share, 2 * latents),
            jnp.broadcast_to(ends[None, None], (8, pad, 2 * latents)),
        ],
        axis=1,
    )
    summed = parts[:4] + partner(parts[4:], "core", 1)
    summed = after(summed, other[2][2])
    summed = scatter_y(summed, F32)
    mine, theirs = summed[:, :latents], summed[:, latents:]
    side_sum = mine + partner(theirs, "xl", 1)
    summed = side_sum + (partner(mine, "xh", 1) + partner(theirs, ("xh", "xl"), 3))
    norm_sum = summed[share]
    preact = summed[:share] + enc_bias[None, :]
    squash = jax.nn.sigmoid(SHARPNESS * preact)
    feature = preact * squash

    block = jnp.concatenate(
        [feature.astype(BF16), jnp.stack(split3(norm)), jnp.zeros((2 * pad - 3, latents), BF16)]
    )
    block, dec_left = lax.optimization_barrier((block, dec_left))
    block = jnp.broadcast_to(block[None], (8, *block.shape))
    other = cross(pieces[5:6], block)
    block = after(lax.all_to_all(block, "z", 0, 0, tiled=True), other[0][2])
    others += other
    dec_right = after(dec_right, block)
    dec_right = lax.all_to_all(dec_right, LATENT, 0, 0, tiled=True)
    block = double(block, "xl", 1, 1).reshape(16, share + 2 * pad, latents)
    norm_rows = jnp.sum(block[:, share : share + 3].astype(F32), axis=1).reshape(-1)
    block = jnp.swapaxes(block[:, :share], 0, 1).reshape(share, -1)
    here = gather_y(block)
    features = here, partner(here, "core", 1)
    mass = sum(jnp.sum(f.astype(F32), axis=0) for f in features)
    coef = (PENALTY_WEIGHT / tokens * mass / norm_rows)[:, None]

    side = width // 2
    parts = [part.reshape(16 * latents, side) for part in (dec_left, dec_right)]
    errors = [None, None]
    errors[1], give, bias, squares = decode(
        features[1], parts, acts_here[half:], dec_bias, tokens, BF16
    )
    errors[0], keep, more_bias, more_squares = decode(
        features[0], parts, acts_here[:half], dec_bias, tokens, F32
    )
    grad_dec_bias = more_bias + bias
    squares += more_squares
    keep += partner(give, "core", 1).astype(F32)
    keep, *errors = lax.optimization_barrier((keep, *errors))
    grads = []
    for i, part in enumerate(parts):
        grad = coef * part.astype(F32)
        for j, f in enumerate(features):
            error = errors[j][:, i * side : (i + 1) * side]
            grad += lax.dot_general(
                f, error, (((0,), (0,)), ((), ())), preferred_element_type=F32
            )
        grads.append(grad.astype(BF16).reshape(16, latents, side))
    grad_left = lax.all_to_all(grads[0], LATENT, 0, 0, tiled=True)

    other = cross(pieces[6:7], keep)
    mine = scatter_y(keep.reshape(4, share, -1), BF16, other[0][2])
    mine = mine.reshape(2, small, -1)
    others += other
    give = lax.dynamic_index_in_dim(mine, 1 - xh, 0, keepdims=False).astype(BF16)
    mine = lax.dynamic_index_in_dim(mine, xh, 0, keepdims=False)
    mine += partner(give, "xh", 1).astype(F32)

    def local(value):
        return lax.dynamic_slice_in_dim(value, xh * small, small, 0)

    preact, squash, feature = local(preact), local(squash), local(feature)
    penalty = jnp.sum(feature * norm_sum[None, :])
    loss = (jnp.sum(squares) + PENALTY_WEIGHT * penalty) / tokens
    mine = jnp.concatenate(
        [
            jnp.swapaxes(mine.reshape(small, 16, latents), 0, 1),
            jnp.broadcast_to(loss, (16, pad, latents)),
        ],
        axis=1,
    )
    mine = halve(mine.reshape(8, 2, small + pad, latents), "xl", 1, 1)
    mine, grad_left, grads[1] = lax.optimization_barrier((mine, grad_left, grads[1]))
    mine = jnp.sum(lax.all_to_all(mine, "z", 0, 0, tiled=True), axis=0)
    grad_right = after(grads[1], mine)
    grad_right = lax.all_to_all(grad_right, LATENT, 0, 0, tiled=True)
    grad_feature = mine[:small] + PENALTY_WEIGHT / tokens * norm_sum[None, :]
    grad_preact = grad_feature * (squash + SHARPNESS * preact * squash * (1.0 - squash))
    block = jnp.concatenate(
        [
            grad_preact.astype(BF16),
            jnp.stack(split3(jnp.sum(grad_preact, axis=0)) + split3(mine[small])),
            jnp.zeros((pad - 6, latents), BF16),
        ]
    )
    near, side_near = partner(block, "xh", 1), partner(block, ("xh", "xl"), 3)
    pair = jnp.stack([block, partner(block, "xl", 1)])
    near = jnp.stack([near, side_near])
    block = jnp.stack([jnp.where(xh == 0, pair, near), jnp.where(xh == 0, near, pair)])
    block = gather_y(block)
    block = jnp.concatenate([block, partner(block, "core", 1)])
    low_side = block[:, 1, :small].reshape(tokens, latents)
    block = block[:, 0]
    ends = block[:, small:].astype(F32).reshape(2, 4, 2, pad, latents)
    ends = jnp.where(core == 0, ends, ends[::-1])
    ends = lax.dynamic_slice_in_dim(jnp.concatenate([ends, ends], axis=1), (4 - y) % 4, 4, 1)
    ends = jnp.sum(ends.reshape(16, pad, latents), axis=0)
    grad_enc_bias = ends[0] + ends[1] + ends[2]
    objective = (ends[3] + ends[4] + ends[5])[0]
    grad_low = block[:, :small].reshape(tokens, latents)
    remote = [pieces[i] for i in (3, 4, 7, 8)]
    came = shift(encode_rows([piece[2] for piece in remote], low_side), "xl", 1)
    grad_enc = encode_grad(z, xl, grad_low, pieces, others, width)
    grad_dec = join_dec(grad_left, grad_right)[:, None]
    came, grad_dec = lax.optimization_barrier((came, grad_dec))
    start = 0
    for dz, row, chunk in remote:
        count = chunk.shape[0]
        place = ((z + dz) % 8 * 2 + 1 - xl) * width + row
        rows = came[start : start + count]
        grad_enc = lax.dynamic_update_slice_in_dim(grad_enc, rows, place, 0)
        start += count
    return objective, grad_enc[None], grad_enc_bias, grad_dec, grad_dec_bias


def solution(mesh):
    fine = Mesh(mesh.devices.reshape(4, 2, 2, 8, 2), LAYER + LATENT)
    placed = (
        P(LAYER, None, LATENT),
        P(LAYER, None, LATENT),
        P(LATENT),
        P(LATENT, LAYER, None),
        P(LAYER, LATENT),
    )
    return jax.shard_map(
        body,
        mesh=fine,
        in_specs=placed,
        out_specs=(
            P(),
            P(LAYER, None, LATENT),
            P(LATENT),
            P(LATENT, LAYER, None),
            P(LAYER, LATENT),
        ),
        check_vma=False,
    )
```

```python
import functools

import jax
import jax.numpy as jnp
from jax import lax
from jax.experimental import pallas as pl
from jax.experimental.pallas import tpu as pltpu
from jax.sharding import Mesh, PartitionSpec as P

SHARPNESS = 4.0
PENALTY_WEIGHT = 4.0
EPSILON = 1e-06

LAYER = ("y", "xh", "core")
LATENT = ("z", "xl")
BF16 = jnp.bfloat16
F32 = jnp.float32


def after(value, *others):
    return lax.optimization_barrier((value, *others))[0]


def shift(value, axis, step):
    size = lax.axis_size(axis)
    return lax.ppermute(value, axis, [(i, (i + step) % size) for i in range(size)])


def partner(value, axis, bit):
    size = lax.axis_size(axis)
    return lax.ppermute(value, axis, [(i, i ^ bit) for i in range(size)])


def bit_of(axis, bit):
    return (lax.axis_index(axis) // bit) % 2


def double(value, axis, bit, dim, *along):
    other = after(partner(value, axis, bit), *along)
    first = bit_of(axis, bit) == 0
    return jnp.stack([jnp.where(first, value, other), jnp.where(first, other, value)], axis=dim)


def halve(value, axis, bit, dim):
    here = bit_of(axis, bit)
    give = lax.dynamic_index_in_dim(value, 1 - here, dim, keepdims=False)
    keep = lax.dynamic_index_in_dim(value, here, dim, keepdims=False)
    return keep + partner(give, axis, bit)


def scatter_y(blocks, kind, *along):
    total = blocks[0].astype(F32)
    came = [shift(blocks[k].astype(kind), "y", k) for k in (2, 1, 3)]
    came[0] = after(came[0], *along)
    for part in came:
        total += part.astype(F32)
    return total


def gather_y(block, *along):
    far, near, last = (shift(block, "y", -k) for k in (2, 1, 3))
    return jnp.concatenate([block, near, after(far, *along), last])


def split3(value):
    high = lax.reduce_precision(value, 8, 7)
    rest = value - high
    middle = lax.reduce_precision(rest, 8, 7)
    return [v.astype(BF16) for v in (high, middle, rest - middle)]


def own_kernel(share, place_ref, acts_ref, rows_ref, turned_ref):
    core, y = place_ref[0], place_ref[1]
    for i in range(8):
        c, k = i // 4, i % 4
        source = ((core + c) % 2 * 4 + (y + k) % 4) * share
        rows_ref[i * share : (i + 1) * share, :] = acts_ref[
            pl.ds(pl.multiple_of(source, share), share), :
        ]
    turned_ref[...] = rows_ref[...].T


def arrange_own(own, core, y):
    tokens, width = own.shape
    return pl.pallas_call(
        functools.partial(own_kernel, tokens // 8),
        in_specs=[
            pl.BlockSpec(memory_space=pltpu.SMEM),
            pl.BlockSpec(memory_space=pltpu.VMEM),
        ],
        out_shape=(
            jax.ShapeDtypeStruct((tokens, width), BF16),
            jax.ShapeDtypeStruct((width, tokens), BF16),
        ),
        name="arrange_own",
    )(jnp.stack([core, y]).astype(jnp.int32), own)


def cut_kernel(dec_ref, left_ref, right_ref):
    half = left_ref.shape[2]
    for i in range(4):
        left_ref[i] = dec_ref[:, 2 * i * half : (2 * i + 1) * half]
        right_ref[i] = dec_ref[:, (2 * i + 1) * half : (2 * i + 2) * half]


def cut_dec(dec, width):
    latents, depth = dec.shape
    count, half = depth // width, width // 2
    piece = pl.BlockSpec((4, latents, half), lambda j: (j, 0, 0))
    shape = jax.ShapeDtypeStruct((count, latents, half), BF16)
    return pl.pallas_call(
        cut_kernel,
        grid=(count // 4,),
        in_specs=[pl.BlockSpec((latents, 4 * width), lambda j: (0, j))],
        out_specs=(piece, piece),
        out_shape=(shape, shape),
        name="cut_dec",
    )(dec)


def join_kernel(left_ref, right_ref, out_ref):
    count, _, side = left_ref.shape
    for i in range(count):
        start = 2 * i * side
        out_ref[:, start : start + side] = left_ref[i]
        out_ref[:, start + side : start + 2 * side] = right_ref[i]


def join_dec(left, right):
    count, latents, side = left.shape
    return pl.pallas_call(
        join_kernel,
        out_shape=jax.ShapeDtypeStruct((latents, 2 * count * side), BF16),
        compiler_params=pltpu.CompilerParams(vmem_limit_bytes=48 * 1024 * 1024),
        name="join_dec",
    )(left, right)


def rows_kernel(low_ref, *refs):
    start = 0
    for chunk_ref in refs[:-1]:
        count = chunk_ref.shape[0]
        rows = jnp.dot(chunk_ref[...], low_ref[...], preferred_element_type=F32)
        refs[-1][start : start + count, :] = rows.astype(BF16)
        start += count


def encode_rows(chunks, low):
    count = sum(chunk.shape[0] for chunk in chunks)
    return pl.pallas_call(
        rows_kernel,
        out_shape=jax.ShapeDtypeStruct((count, low.shape[1]), BF16),
        compiler_params=pltpu.CompilerParams(vmem_limit_bytes=48 * 1024 * 1024),
        name="encode_rows",
    )(low, *chunks)


def grad_enc_kernel(width, steps, place_ref, low_ref, *refs):
    z, xl = place_ref[0], place_ref[1]
    out_ref = refs[-1]
    for (dz, dx, row), chunk_ref in zip(steps, refs):
        place = ((z + dz + 8) % 8 * 2 + (xl + dx) % 2) * width + row
        count = chunk_ref.shape[0]
        rows = jnp.dot(chunk_ref[...], low_ref[...], preferred_element_type=F32)
        out_ref[pl.ds(pl.multiple_of(place, count), count), :] = rows.astype(BF16)


def encode_grad(z, xl, low, pieces, others, width):
    steps = [(dz, 0, row) for dz, row, _ in pieces] + [(dz, 1, row) for dz, row, _ in others]
    chunks = [piece[2] for piece in (*pieces, *others)]
    specs = [pl.BlockSpec(memory_space=pltpu.SMEM)]
    specs += [pl.BlockSpec(memory_space=pltpu.VMEM)] * (1 + len(chunks))
    return pl.pallas_call(
        functools.partial(grad_enc_kernel, width, steps),
        in_specs=specs,
        out_shape=jax.ShapeDtypeStruct((16 * width, low.shape[1]), BF16),
        compiler_params=pltpu.CompilerParams(vmem_limit_bytes=48 * 1024 * 1024),
        name="encode_grad",
    )(jnp.stack([z, xl]).astype(jnp.int32), low, *chunks)


def decode_kernel(scale, here, there, left, right, acts, shift_ref, *outs):
    scaled_here, scaled_there, keep, give, bias, squares = outs
    half, side = here.shape[0], left.shape[1]
    rows = half // 2
    bias[...] = jnp.zeros_like(bias)
    squares[...] = jnp.zeros_like(squares)
    steps = (here, keep, scaled_here), (there, give, scaled_there)
    for j, (features, out, scaled) in enumerate(steps):
        for r in range(0, half, rows):
            f = features[r : r + rows, :]
            lines = slice(j * half + r, j * half + r + rows)
            products = []
            for i, part in enumerate((left, right)):
                columns = slice(i * side, (i + 1) * side)
                rebuilt = jnp.dot(f, part[...], preferred_element_type=F32)
                error = rebuilt + shift_ref[:, columns] - acts[lines, columns].astype(F32)
                wide = scale * error
                low = wide.astype(BF16)
                scaled[r : r + rows, columns] = low
                bias[:, columns] += jnp.sum(wide, axis=0, keepdims=True)
                squares[:, columns] += jnp.sum(error * error, axis=0, keepdims=True)
                products.append(
                    lax.dot_general(
                        low, part[...], (((1,), (1,)), ((), ())), preferred_element_type=F32
                    )
                )
            out[r : r + rows, :] = (products[0] + products[1]).astype(out.dtype)


def decode(features, parts, acts, shifts, tokens):
    half, total = features[0].shape
    width = acts.shape[1]
    return pl.pallas_call(
        functools.partial(decode_kernel, 2.0 / tokens),
        out_shape=(
            jax.ShapeDtypeStruct((half, width), BF16),
            jax.ShapeDtypeStruct((half, width), BF16),
            jax.ShapeDtypeStruct((half, total), F32),
            jax.ShapeDtypeStruct((half, total), BF16),
            jax.ShapeDtypeStruct((1, width), F32),
            jax.ShapeDtypeStruct((1, width), F32),
        ),
        compiler_params=pltpu.CompilerParams(vmem_limit_bytes=48 * 1024 * 1024),
        cost_estimate=pl.CostEstimate(
            flops=8 * half * total * width,
            transcendentals=0,
            bytes_accessed=16 * half * total,
        ),
        name="decode",
    )(*features, *parts, acts, shifts)


def gather_acts(own, slab, early, use, state):
    half = own.shape[0] // 2
    up, down = shift(own, "z", 1), shift(own, "z", -1)
    xl = lax.axis_index("xl")
    came = shift(lax.dynamic_index_in_dim(slab, 1 - xl, 1, keepdims=False), "xl", 1)
    first = [(0, 0, own), (-1, 0, up), (1, 0, down)]
    other = [(k, 0, shift(after(v, came), "xl", 1)) for k, _, v in first]
    up, down, *early = lax.optimization_barrier((up, down, *early))
    up, down = shift(up, "z", 1), shift(down, "z", -1)
    slab = lax.dynamic_index_in_dim(after(slab, came), xl, 1, keepdims=False)
    slab = jnp.concatenate([slab, came], axis=2)
    state = use(state, first, slab)
    second = [(-2, 0, up), (2, 0, down)]
    up, down, state = lax.optimization_barrier((up, down, state))
    up, down = shift(up, "z", 1), shift(down, "z", -1)
    state = use(state, second, slab)
    third = [(-3, 0, up), (3, 0, down)]
    up, down, state = lax.optimization_barrier((up, down, state))
    top, bottom = lax.optimization_barrier((up[:half], down[half:]))
    far = [(4, 0, shift(top, "z", 1)), (4, half, shift(bottom, "z", -1))]
    state = use(state, third, slab)
    early[0] = after(early[0], state)
    state = use(state, far, slab)
    return state, first + second + third + far, other, early


def body(activations, enc_weight, enc_bias, dec_weight, dec_bias):
    tokens, width = activations.shape[1:]
    latents = enc_weight.shape[2]
    half, share = tokens // 2, tokens // 8
    small = share // 2
    pad = 8
    enc = enc_weight[0]
    dec = dec_weight[:, 0]
    z, xl, core, xh, y = (lax.axis_index(a) for a in ("z", "xl", "core", "xh", "y"))

    acts_here, turned = arrange_own(activations[0], core, y)
    def use(total, pieces, slab):
        for dz, row, chunk in pieces:
            rows = lax.dynamic_index_in_dim(slab, (z + dz) % 8, 0, keepdims=False)
            rows = rows[row : row + chunk.shape[0]]
            total += lax.dot_general(
                chunk, rows, (((0,), (0,)), ((), ())), preferred_element_type=F32
            )
        return total

    def cross(pieces, *others):
        return [(k, row, shift(after(v, *others), "xl", 1)) for k, row, v in pieces]

    wide = dec.astype(F32)
    norm = jnp.sqrt(jnp.sum(wide * wide, axis=1) + EPSILON)
    slab = after(enc, turned).reshape(8, 2, width, latents)
    total = jnp.zeros((tokens, 2 * latents), F32)
    early = [*cut_dec(dec, width), norm]
    total, pieces, other, early = gather_acts(turned, slab, early, use, total)
    others = list(other)
    dec_left, dec_right, norm = early
    total = after(total, other[0][2], other[1][2])
    dec_left = lax.all_to_all(dec_left, LATENT, 0, 0, tiled=True)

    ends = jnp.concatenate([norm, jnp.zeros_like(norm)])
    parts = jnp.concatenate(
        [
            total.reshape(8, share, 2 * latents),
            jnp.broadcast_to(ends[None, None], (8, pad, 2 * latents)),
        ],
        axis=1,
    )
    summed = parts[:4] + partner(parts[4:], "core", 1)
    summed = after(summed, other[2][2])
    summed = scatter_y(summed, F32)
    mine, theirs = summed[:, :latents], summed[:, latents:]
    side_sum = mine + partner(theirs, "xl", 1)
    summed = side_sum + (partner(mine, "xh", 1) + partner(theirs, ("xh", "xl"), 3))
    norm_sum = summed[share]
    preact = summed[:share] + enc_bias[None, :]
    squash = jax.nn.sigmoid(SHARPNESS * preact)
    feature = preact * squash

    block = jnp.concatenate(
        [feature.astype(BF16), jnp.stack(split3(norm)), jnp.zeros((2 * pad - 3, latents), BF16)]
    )
    block, dec_left = lax.optimization_barrier((block, dec_left))
    block = jnp.broadcast_to(block[None], (8, *block.shape))
    low = width // 2
    k, _, chunk = pieces[5]
    split = [(k, 0, chunk[:low]), (k, low, chunk[low:])]
    other = cross(split[:1], block)
    block = after(lax.all_to_all(block, "z", 0, 0, tiled=True), other[0][2])
    others += other
    dec_right = after(dec_right, block)
    dec_right = lax.all_to_all(dec_right, LATENT, 0, 0, tiled=True)
    block = double(block, "xl", 1, 1).reshape(16, share + 2 * pad, latents)
    norm_rows = jnp.sum(block[:, share : share + 3].astype(F32), axis=1).reshape(-1)
    block = jnp.swapaxes(block[:, :share], 0, 1).reshape(share, -1)
    other = cross(split[1:], block)
    here = gather_y(block, other[0][2])
    others += other
    features = here, partner(here, "core", 1)
    mass = sum(jnp.sum(f.astype(F32), axis=0) for f in features)
    coef = (PENALTY_WEIGHT / tokens * mass / norm_rows)[:, None]

    dec_right, coef = lax.optimization_barrier((dec_right, coef))
    side = width // 2
    parts = [part.reshape(16 * latents, side) for part in (dec_left, dec_right)]
    *errors, keep, give, grad_dec_bias, squares = decode(
        features, parts, acts_here, dec_bias, tokens
    )
    keep += partner(give, "core", 1).astype(F32)
    keep, *errors = lax.optimization_barrier((keep, *errors))
    grads = []
    for i, part in enumerate(parts):
        grad = coef * part.astype(F32)
        for j, f in enumerate(features):
            error = errors[j][:, i * side : (i + 1) * side]
            grad += lax.dot_general(
                f, error, (((0,), (0,)), ((), ())), preferred_element_type=F32
            )
        grads.append(grad.astype(BF16).reshape(16, latents, side))
    grad_left = lax.all_to_all(grads[0], LATENT, 0, 0, tiled=True)

    other = cross(pieces[6:7], keep)
    mine = scatter_y(keep.reshape(4, share, -1), BF16, other[0][2])
    mine = mine.reshape(2, small, -1)
    others += other
    give = lax.dynamic_index_in_dim(mine, 1 - xh, 0, keepdims=False).astype(BF16)
    mine = lax.dynamic_index_in_dim(mine, xh, 0, keepdims=False)
    mine += partner(give, "xh", 1).astype(F32)

    def local(value):
        return lax.dynamic_slice_in_dim(value, xh * small, small, 0)

    preact, squash, feature = local(preact), local(squash), local(feature)
    penalty = jnp.sum(feature * norm_sum[None, :])
    loss = (jnp.sum(squares) + PENALTY_WEIGHT * penalty) / tokens
    mine = jnp.concatenate(
        [
            jnp.swapaxes(mine.reshape(small, 16, latents), 0, 1),
            jnp.broadcast_to(loss, (16, pad, latents)),
        ],
        axis=1,
    )
    mine = halve(mine.reshape(8, 2, small + pad, latents), "xl", 1, 1)
    mine, grad_left, grads[1] = lax.optimization_barrier((mine, grad_left, grads[1]))
    mine = jnp.sum(lax.all_to_all(mine, "z", 0, 0, tiled=True), axis=0)
    grad_right = after(grads[1], mine)
    grad_right = lax.all_to_all(grad_right, LATENT, 0, 0, tiled=True)
    grad_feature = mine[:small] + PENALTY_WEIGHT / tokens * norm_sum[None, :]
    grad_preact = grad_feature * (squash + SHARPNESS * preact * squash * (1.0 - squash))
    block = jnp.concatenate(
        [
            grad_preact.astype(BF16),
            jnp.stack(split3(jnp.sum(grad_preact, axis=0)) + split3(mine[small])),
            jnp.zeros((pad - 6, latents), BF16),
        ]
    )
    near, side_near = partner(block, "xh", 1), partner(block, ("xh", "xl"), 3)
    pair = jnp.stack([block, partner(block, "xl", 1)])
    near = jnp.stack([near, side_near])
    block = jnp.stack([jnp.where(xh == 0, pair, near), jnp.where(xh == 0, near, pair)])
    block = gather_y(block)
    block = jnp.concatenate([block, partner(block, "core", 1)])
    low_side = block[:, 1, :small].reshape(tokens, latents)
    block = block[:, 0]
    ends = block[:, small:].astype(F32).reshape(2, 4, 2, pad, latents)
    ends = jnp.where(core == 0, ends, ends[::-1])
    ends = lax.dynamic_slice_in_dim(jnp.concatenate([ends, ends], axis=1), (4 - y) % 4, 4, 1)
    ends = jnp.sum(ends.reshape(16, pad, latents), axis=0)
    grad_enc_bias = ends[0] + ends[1] + ends[2]
    objective = (ends[3] + ends[4] + ends[5])[0]
    grad_low = block[:, :small].reshape(tokens, latents)
    remote = [pieces[i] for i in (3, 4, 7, 8)]
    came = shift(encode_rows([piece[2] for piece in remote], low_side), "xl", 1)
    grad_enc = encode_grad(z, xl, grad_low, pieces, others, width)
    grad_dec = join_dec(grad_left, grad_right)[:, None]
    came, grad_dec = lax.optimization_barrier((came, grad_dec))
    start = 0
    for dz, row, chunk in remote:
        count = chunk.shape[0]
        place = ((z + dz) % 8 * 2 + 1 - xl) * width + row
        rows = came[start : start + count]
        grad_enc = lax.dynamic_update_slice_in_dim(grad_enc, rows, place, 0)
        start += count
    return objective, grad_enc[None], grad_enc_bias, grad_dec, grad_dec_bias


def solution(mesh):
    fine = Mesh(mesh.devices.reshape(4, 2, 2, 8, 2), LAYER + LATENT)
    placed = (
        P(LAYER, None, LATENT),
        P(LAYER, None, LATENT),
        P(LATENT),
        P(LATENT, LAYER, None),
        P(LAYER, LATENT),
    )
    return jax.shard_map(
        body,
        mesh=fine,
        in_specs=placed,
        out_specs=(
            P(),
            P(LAYER, None, LATENT),
            P(LATENT),
            P(LATENT, LAYER, None),
            P(LAYER, LATENT),
        ),
        check_vma=False,
    )
```
